32 devices in a mesh: cfg: 2 (over y), src: 8 (over z, core), snk: 2 (over x), spin: 1.
Axes of the slice: x: 2, y: 2, z: 4, core: 2. Of those that a mesh axis runs over, the one named last changes fastest.
Arguments:
- src_times: int32 [8], P('src'), may hold values from 0 to 31, as said below
- momenta: int32 [8, 2], P('src'), may hold values from 0 to 1
- band_offsets: int32 [16], P('snk'), may hold values from 0 to 15, as said below
- elementals: bfloat16 [4, 32, 2, 128, 128], P('cfg', 'src'), parts along dimension 0, may hold values from -0.5 to 0.5
- perambulators: bfloat16 [16, 16, 2, 512, 512], P(('cfg', 'src'), 'snk', None, None, 'spin'), parts along dimension 0, may hold values from -1.1953125 to 1.1953125
Outputs:
- trace_terms: float32 [16, 16, 2, 512], P(('cfg', 'src'), 'snk', None, 'spin'), parts along dimension 0
- correlator: float32 [16, 16, 2], P(('cfg', 'src'), 'snk'), parts along dimension 0
The draws below stay inside these ranges and needn't reach their ends.
There are 2 independent parts, one for each index of `cfg`. The reference program is written for one: setup_inputs(seed, part) draws one part's arguments, and reference() takes and returns one part's arrays. A program takes and returns all parts, laid end to end along the dimension named above; an argument that names none is the same for every part. Nothing has to cross between parts.
Inputs may be any that keep to these rules, and one draw needn't show every extreme that they name: src_times[s] lies in [s * 4, (s + 1) * 4); the first and the last source sit at the last slice of their tile. `band_offsets`: each offset appears once.
All inputs are finite; a program needn't handle non-finite values.
Results may differ from the reference program's by a relative error of at most 0.014.
Values may be sent and summed in bfloat16 or wider, within the bound.
A program may use at most 128 MiB of HBM per device.

```python
import jax
import jax.numpy as jnp
from jax import lax

EIG = 128
ROWS = 512
NMOM = 2
TIME_DEV = 4
NSRC = 8
BANDN = 16
NT = 32


def draw_src_times(key, part):
    key = jax.random.fold_in(key, 11)
    jitter = jax.random.randint(key, (NSRC,), 0, TIME_DEV)
    order = jnp.arange(NSRC, dtype=jnp.int32)
    jitter = jnp.where(order == 0, TIME_DEV - 1, jitter)
    jitter = jnp.where(order == NSRC - 1, TIME_DEV - 1, jitter)
    return (order * TIME_DEV + jitter).astype(jnp.int32)


def draw_band_offsets(key, part):
    key = jax.random.fold_in(key, 23)
    return jax.random.permutation(key, BANDN).astype(jnp.int32)


def set_ends(result, key, low, top_value):
    longest = result.shape.index(max(result.shape))
    spots = []
    for shift in (0, 1):
        where = [jax.random.randint(jax.random.fold_in(key, axis), (), 0, length) for axis, length in enumerate(result.shape)]
        where[longest] = (where[longest] + shift) % result.shape[longest]
        spots.append(tuple(where))
    return result.at[spots[0]].set(low).at[spots[1]].set(top_value)


def levels(own_key, extent, cuts, smallest, high):
    loudness = 1.0
    for dim, shards_of in cuts:
        draws = jax.random.uniform(jax.random.fold_in(jax.random.fold_in(own_key, 6), dim), (shards_of,), jnp.float32, smallest / len(cuts), high / len(cuts))
        loudness = loudness * jnp.repeat(jnp.exp(draws), extent[dim] // shards_of).reshape((-1,) + (1,) * (len(extent) - 1 - dim))
    return loudness


def scatter_about(stream_key, extent, scale, reach, pieces=(), kind=jnp.bfloat16):
    entries = jax.random.normal(stream_key, extent, jnp.float32) * scale
    if len(pieces) > 0:
        entries = levels(stream_key, extent, pieces, -0.22, 0.18) * entries
    return jnp.clip(entries, min=-reach, max=reach).astype(kind)


def setup_inputs(seed: int = 0, part: int = 0) -> dict:
    keys = jax.random.split(jax.random.key(seed), 6)
    own_keys = jax.random.split(jax.random.fold_in(keys[5], part), 6)
    return {
        "src_times": draw_src_times(jax.random.fold_in(keys[5], 71), part),
        "momenta": set_ends(jax.random.randint(keys[1], (NSRC, 2), 0, NMOM), jax.random.fold_in(keys[1], 1), 0, NMOM - 1).astype(jnp.int32),
        "band_offsets": draw_band_offsets(jax.random.fold_in(keys[5], 71), part),
        "elementals": scatter_about(own_keys[3], (NMOM, NT, 2, EIG, EIG), EIG ** -0.5, 0.5, ((1, 8),)),
        "perambulators": scatter_about(own_keys[4], (NSRC, BANDN, 2, ROWS, ROWS), 0.2, 1.1953125, ((0, 8), (1, 2))),
    }


def contract(source_elem, sink_elem, tau):
    width = tau.shape[-1]
    blocks = tau.reshape(2, 4, EIG, width).astype(jnp.float32)
    first = source_elem.astype(jnp.float32)
    second = sink_elem.astype(jnp.float32)

    def rowmul(a, b):
        return jnp.einsum("ab,pbc->pac", a, b, precision=lax.Precision.HIGHEST).reshape(4 * EIG, width)

    left_re = (rowmul(first[0], blocks[0]) - rowmul(first[1], blocks[1])).astype(jnp.bfloat16)
    left_im = (rowmul(first[0], blocks[1]) + rowmul(first[1], blocks[0])).astype(jnp.bfloat16)
    columns = tau.reshape(2, 4 * EIG, width // EIG, EIG).astype(jnp.float32)

    def colmul(a, b):
        return jnp.einsum("ab,iqb->qai", a, b, precision=lax.Precision.HIGHEST).reshape(width, 4 * EIG)

    right_re = (colmul(second[0], columns[0]) + colmul(second[1], columns[1])).astype(jnp.bfloat16)
    right_im = (colmul(second[1], columns[0]) - colmul(second[0], columns[1])).astype(jnp.bfloat16)
    lre = left_re.astype(jnp.float32)
    lim = left_im.astype(jnp.float32)
    rre = right_re.astype(jnp.float32)
    rim = right_im.astype(jnp.float32)
    real_part = jnp.sum(lre * rre.T - lim * rim.T, axis=0)
    imag_part = jnp.sum(lre * rim.T + lim * rre.T, axis=0)
    return jnp.stack([real_part, imag_part])


def reference(src_times, momenta, band_offsets, elementals, perambulators):
    def single(index):
        source = index // BANDN
        entry = index % BANDN
        start = src_times[source]
        finish = (start + band_offsets[entry]) % NT
        source_elem = elementals[momenta[source, 0], start]
        sink_elem = elementals[momenta[source, 1], finish]
        return contract(source_elem, sink_elem, perambulators[source, entry])

    terms = lax.map(single, jnp.arange(NSRC * BANDN, dtype=jnp.int32))
    terms = terms.reshape(NSRC, BANDN, 2, ROWS)
    correlator = jnp.sum(terms, axis=-1) * jnp.float32(ROWS ** -0.5)
    return terms, correlator
```

```python
import functools

import jax
import jax.numpy as jnp
from jax import lax
from jax.experimental import pallas as pl
from jax.experimental.pallas import tpu as pltpu
from jax.sharding import PartitionSpec as P

EIG = 128
ROWS = 512


def from_behind(value, axis, steps):
    count = lax.axis_size(axis)
    pairs = [(source, (source + steps) % count) for source in range(count)]
    return lax.ppermute(value, axis, pairs)


def contract(source_elem, sink_elem, tau):
    width = tau.shape[-1]
    blocks = tau.reshape(2, 4, EIG, width)

    def rowmul(a, b):
        return jnp.einsum("ab,pbc->pac", a, b, preferred_element_type=jnp.float32).reshape(
            4 * EIG, width
        )

    left_re = (rowmul(source_elem[0], blocks[0]) - rowmul(source_elem[1], blocks[1])).astype(
        jnp.bfloat16
    )
    left_im = (rowmul(source_elem[0], blocks[1]) + rowmul(source_elem[1], blocks[0])).astype(
        jnp.bfloat16
    )
    columns = tau.reshape(2, 4 * EIG, width // EIG, EIG)

    def colmul(a, b):
        return jnp.einsum("ab,iqb->qai", a, b, preferred_element_type=jnp.float32).reshape(
            width, 4 * EIG
        )

    right_re = (colmul(sink_elem[0], columns[0]) + colmul(sink_elem[1], columns[1])).astype(
        jnp.bfloat16
    )
    right_im = (colmul(sink_elem[1], columns[0]) - colmul(sink_elem[0], columns[1])).astype(
        jnp.bfloat16
    )
    lre = left_re.astype(jnp.float32)
    lim = left_im.astype(jnp.float32)
    rre = right_re.astype(jnp.float32)
    rim = right_im.astype(jnp.float32)
    real_part = jnp.sum(lre * rre.T - lim * rim.T, axis=0)
    imag_part = jnp.sum(lre * rim.T + lim * rre.T, axis=0)
    return jnp.stack([real_part, imag_part])


def local(src_times, momenta, band_offsets, elementals, perambulators):
    tile = elementals.shape[1]
    first_slice = lax.axis_index("src") * tile
    start = src_times[0] - first_slice
    band_total = band_offsets.shape[0] * lax.axis_size("snk")
    reach = band_total // tile
    source_elem = elementals[momenta[0, 0], start]
    pieces = [elementals]
    for step in range(1, reach + 1):
        pieces.append(from_behind(elementals, "src", -step))
    window = jnp.concatenate(pieces, axis=1)[momenta[0, 1]]
    positions = start + band_offsets
    selector = (positions[:, None] == jnp.arange(window.shape[0], dtype=jnp.int32)[None, :]).astype(
        jnp.bfloat16
    )
    sink_elem = jnp.einsum(
        "ow,wxab->oxab", selector, window, preferred_element_type=jnp.float32
    ).astype(jnp.bfloat16)
    terms = jax.vmap(contract, in_axes=(None, 0, 0))(source_elem, sink_elem, perambulators[0])
    partial_sum = jnp.sum(terms, axis=-1)
    total = lax.psum(partial_sum, "spin")
    correlator = total * jnp.float32(ROWS ** (-0.5))
    return (terms[None], correlator[None])


TILE = 4
NEAR, FAR = 0, 1


def fused_kernel(
    times_ref,
    momenta_ref,
    offsets_ref,
    elem_ref,
    tau_ref,
    terms_ref,
    corr_ref,
    tau,
    own,
    win,
    weight,
    left,
    outer,
    tau_sem,
    own_sem,
    put_sem,
    down_send,
    up_send,
    relay_send,
    z_recv,
    x_send,
    x_recv,
    own_send,
    own_recv,
    pair_send,
    pair_recv,
):
    src = lax.axis_index("src")
    x = lax.axis_index("snk")
    z = lax.div(src, 2)
    c = lax.rem(src, 2)
    entries = tau_ref.shape[0]
    other = 1 - x
    sibling = {"src": src + 1 - 2 * c}
    across = {"snk": other}

    def remote(source, target, send, recv, device):
        return pltpu.make_async_remote_copy(
            src_ref=source,
            dst_ref=target,
            send_sem=send,
            recv_sem=recv,
            device_id=device,
            device_id_type=pl.DeviceIdType.MESH,
        )

    def place(kind, k):
        return (2 + 2 * kind + c) * TILE + k

    own_copy = pltpu.make_async_copy(elem_ref, own, own_sem)
    own_copy.start()
    put_copy = pltpu.make_async_copy(elem_ref, win.at[:, pl.ds(c * TILE, TILE)], put_sem)
    put_copy.start()
    for i in range(entries):
        pltpu.make_async_copy(tau_ref.at[i], tau.at[i], tau_sem.at[i]).start()

    barrier = pltpu.get_barrier_semaphore()

    def greet(device):
        pl.semaphore_signal(barrier, inc=1, device_id=device, device_id_type=pl.DeviceIdType.MESH)

    greet(sibling)
    greet(across)
    has_up = z <= 1

    @pl.when(z >= 1)
    def _():
        greet({"src": src - 2})

    @pl.when(z <= 2)
    def _():
        greet({"src": src + 2})

    @pl.when(has_up)
    def _():
        greet({"src": src + 4})

    @pl.when(z >= 2)
    def _():
        greet({"src": src - 4})

    pl.semaphore_wait(barrier, 4 + jnp.where((z == 1) | (z == 2), 1, 0))

    def down(k):
        return remote(
            elem_ref.at[x, k],
            win.at[x, place(NEAR, k)],
            down_send.at[k],
            z_recv.at[NEAR * TILE + k],
            {"src": src - 2},
        )

    def up(k):
        return remote(
            elem_ref.at[x, k],
            win.at[x, place(FAR, k)],
            up_send.at[k],
            z_recv.at[FAR * TILE + k],
            {"src": src + 4},
        )

    @pl.when(z >= 1)
    def _():
        for k in range(TILE):
            down(k).start()

    @pl.when(has_up)
    def _():
        for k in range(TILE):
            up(k).start()

    def own_push():
        return remote(
            elem_ref, win.at[:, pl.ds(TILE, TILE)], own_send, own_recv, sibling
        )

    @pl.when(c == 1)
    def _():
        own_push().start()

    def step_of(i):
        first = z <= 1
        kind = jnp.where(first, lax.div(i, TILE), lax.rem(i, 2))
        k = jnp.where(first, lax.rem(i, TILE), lax.div(i, 2))
        return kind, k

    def arrival(kind, k):
        slot = win.at[x, place(kind, k)]
        return remote(slot, slot, x_send.at[0], z_recv.at[kind * TILE + k], across)

    def relay_down(k):
        return remote(
            win.at[x, place(NEAR, k)],
            win.at[x, place(FAR, k)],
            relay_send.at[NEAR * TILE + k],
            z_recv.at[FAR * TILE + k],
            {"src": src - 2},
        )

    def relay_up(k):
        return remote(
            win.at[x, place(FAR, k)],
            win.at[x, place(NEAR, k)],
            relay_send.at[FAR * TILE + k],
            z_recv.at[NEAR * TILE + k],
            {"src": src + 2},
        )

    def cross(kind, k, plane):
        slot = win.at[plane, place(kind, k)]
        at = kind * TILE + k
        return remote(slot, slot, x_send.at[at], x_recv.at[at], across)

    def pair(kind, k, plane, hop):
        slot = win.at[plane, place(kind, k)]
        at = (hop * 2 + kind) * TILE + k
        return remote(slot, slot, pair_send.at[at], pair_recv.at[at], sibling)

    def pair_in(kind, k, plane, hop):
        slot = win.at[plane, (2 + 2 * kind + 1 - c) * TILE + k]
        at = (hop * 2 + kind) * TILE + k
        return remote(slot, slot, pair_send.at[at], pair_recv.at[at], sibling)

    own_copy.wait()
    m0 = momenta_ref[0, 0]
    m1 = momenta_ref[0, 1]
    start = lax.rem(times_ref[0], TILE)
    source = own[m0, start]
    weight[:EIG, :EIG] = source[0]
    weight[:EIG, EIG:] = -source[1]
    weight[EIG:, :EIG] = source[1]
    weight[EIG:, EIG:] = source[0]

    def hand_on(i):
        kind, k = step_of(i)
        arrival(kind, k).wait_recv()

        @pl.when((kind == NEAR) & ((z == 1) | (z == 2)))
        def _():
            relay_down(k).start()

        @pl.when((kind == FAR) & (z == 2))
        def _():
            relay_up(k).start()

        cross(kind, k, x).start()

        @pl.when((kind == NEAR) | (c == 0))
        def _():
            pair(kind, k, x, 0).start()

    def hand_across(i):
        kind, k = step_of(i)
        cross(kind, k, other).wait_recv()

        @pl.when((kind == NEAR) | (c == 0))
        def _():
            pair(kind, k, other, 1).start()

    def work(i):
        pltpu.make_async_copy(tau_ref.at[i], tau.at[i], tau_sem.at[i]).wait()
        for a in range(4):
            rows = pl.ds(a * EIG, EIG)
            both = jnp.concatenate([tau[i, 0, rows, :], tau[i, 1, rows, :]], axis=0)
            product = jnp.dot(weight[...], both, preferred_element_type=jnp.float32)
            product = product.astype(jnp.bfloat16)
            left[0, rows, :] = product[:EIG]
            left[1, rows, :] = product[EIG:]
        for p in range(4):
            cols = pl.ds(p * EIG, EIG)
            t = jnp.concatenate([tau[i, 0, :, cols], tau[i, 1, :, cols]], axis=1)
            l = jnp.concatenate([left[0, :, cols], left[1, :, cols]], axis=1)
            q = lax.dot_general(
                t, l, (((0,), (0,)), ((), ())), preferred_element_type=jnp.float32
            )
            outer[i, p, 0] = q[:EIG, :EIG] + q[EIG:, EIG:]
            outer[i, p, 1] = q[:EIG, EIG:] - q[EIG:, :EIG]

    @pl.loop(0, entries)
    def _(i):
        hand_on(i)

        @pl.when(i >= 1)
        def _():
            hand_across(i - 1)

        work(i)

    hand_across(entries - 1)

    put_copy.wait()

    @pl.when(c == 0)
    def _():
        own_push().wait_recv()

    @pl.when(c == 1)
    def _():
        own_push().wait_send()

    for kind in (NEAR, FAR):
        for k in range(TILE):
            if kind == NEAR:
                pair_in(kind, k, x, 0).wait_recv()
                pair_in(kind, k, other, 1).wait_recv()
            else:

                @pl.when(c == 1)
                def _():
                    pair_in(kind, k, x, 0).wait_recv()
                    pair_in(kind, k, other, 1).wait_recv()

    def finish(o):
        sink = win[m1, c * TILE + start + offsets_ref[o]]
        er = sink[0].astype(jnp.float32).T
        ei = sink[1].astype(jnp.float32).T
        for p in range(4):
            mr = outer[o, p, 0]
            mi = outer[o, p, 1]
            cols = pl.ds(p * EIG, EIG)
            terms_ref[o, 0:1, cols] = jnp.sum(er * mr - ei * mi, axis=0, keepdims=True)
            terms_ref[o, 1:2, cols] = jnp.sum(er * mi + ei * mr, axis=0, keepdims=True)

    @pl.loop(0, entries)
    def _(o):
        finish(o)

    corr_ref[...] = jnp.sum(terms_ref[...], axis=-1) * jnp.float32(ROWS ** (-0.5))

    @pl.when(z >= 1)
    def _():
        for k in range(TILE):
            down(k).wait_send()

    @pl.when(has_up)
    def _():
        for k in range(TILE):
            up(k).wait_send()

    @pl.when((z == 1) | (z == 2))
    def _():
        for k in range(TILE):
            relay_down(k).wait_send()

    @pl.when(z == 2)
    def _():
        for k in range(TILE):
            relay_up(k).wait_send()

    for kind in (NEAR, FAR):
        for k in range(TILE):
            cross(kind, k, x).wait_send()
            if kind == NEAR:
                pair(kind, k, x, 0).wait_send()
                pair(kind, k, other, 1).wait_send()
            else:

                @pl.when(c == 0)
                def _():
                    pair(kind, k, x, 0).wait_send()
                    pair(kind, k, other, 1).wait_send()


def fused_local(src_times, momenta, band_offsets, elementals, perambulators):
    entries = band_offsets.shape[0]
    bf16 = jnp.bfloat16
    dma = pltpu.SemaphoreType.DMA
    smem = pl.BlockSpec(memory_space=pltpu.SMEM)
    hbm = pl.BlockSpec(memory_space=pl.ANY)
    vmem = pl.BlockSpec(memory_space=pltpu.VMEM)
    terms, correlator = pl.pallas_call(
        fused_kernel,
        out_shape=(
            jax.ShapeDtypeStruct((entries, 2, ROWS), jnp.float32),
            jax.ShapeDtypeStruct((entries, 2), jnp.float32),
        ),
        in_specs=[smem, smem, smem, hbm, hbm],
        out_specs=(vmem, vmem),
        scratch_shapes=[
            pltpu.VMEM((entries, 2, ROWS, ROWS), bf16),
            pltpu.VMEM((2, TILE, 2, EIG, EIG), bf16),
            pltpu.VMEM((2, 6 * TILE, 2, EIG, EIG), bf16),
            pltpu.VMEM((2 * EIG, 2 * EIG), bf16),
            pltpu.VMEM((2, ROWS, ROWS), bf16),
            pltpu.VMEM((entries, 4, 2, EIG, EIG), jnp.float32),
            dma((entries,)),
            dma,
            dma,
            dma((TILE,)),
            dma((TILE,)),
            dma((2 * TILE,)),
            dma((2 * TILE,)),
            dma((2 * TILE,)),
            dma((2 * TILE,)),
            dma,
            dma,
            dma((4 * TILE,)),
            dma((4 * TILE,)),
        ],
        compiler_params=pltpu.CompilerParams(
            collective_id=0, has_side_effects=True, vmem_limit_bytes=60 * 1024 * 1024
        ),
        name="band_contraction",
    )(src_times, momenta, band_offsets, elementals, perambulators[0])
    return terms[None], correlator[None]


def solution(mesh):
    placed = (
        P("src"),
        P("src", None),
        P("snk"),
        P("cfg", "src", None, None, None),
        P(("cfg", "src"), "snk", None, None, "spin"),
    )
    inside = local
    if dict(mesh.shape) == {"cfg": 2, "src": 8, "snk": 2, "spin": 1}:
        inside = fused_local
    return jax.shard_map(
        inside,
        mesh=mesh,
        in_specs=placed,
        out_specs=(P(("cfg", "src"), "snk", None, "spin"), P(("cfg", "src"), "snk", None)),
        check_vma=False,
    )
```

```python
import functools

import jax
import jax.numpy as jnp
from jax import lax
from jax.experimental import pallas as pl
from jax.experimental.pallas import tpu as pltpu
from jax.sharding import PartitionSpec as P

EIG = 128
ROWS = 512


def from_behind(value, axis, steps):
    count = lax.axis_size(axis)
    pairs = [(source, (source + steps) % count) for source in range(count)]
    return lax.ppermute(value, axis, pairs)


def contract(source_elem, sink_elem, tau):
    width = tau.shape[-1]
    blocks = tau.reshape(2, 4, EIG, width)

    def rowmul(a, b):
        return jnp.einsum("ab,pbc->pac", a, b, preferred_element_type=jnp.float32).reshape(
            4 * EIG, width
        )

    left_re = (rowmul(source_elem[0], blocks[0]) - rowmul(source_elem[1], blocks[1])).astype(
        jnp.bfloat16
    )
    left_im = (rowmul(source_elem[0], blocks[1]) + rowmul(source_elem[1], blocks[0])).astype(
        jnp.bfloat16
    )
    columns = tau.reshape(2, 4 * EIG, width // EIG, EIG)

    def colmul(a, b):
        return jnp.einsum("ab,iqb->qai", a, b, preferred_element_type=jnp.float32).reshape(
            width, 4 * EIG
        )

    right_re = (colmul(sink_elem[0], columns[0]) + colmul(sink_elem[1], columns[1])).astype(
        jnp.bfloat16
    )
    right_im = (colmul(sink_elem[1], columns[0]) - colmul(sink_elem[0], columns[1])).astype(
        jnp.bfloat16
    )
    lre = left_re.astype(jnp.float32)
    lim = left_im.astype(jnp.float32)
    rre = right_re.astype(jnp.float32)
    rim = right_im.astype(jnp.float32)
    real_part = jnp.sum(lre * rre.T - lim * rim.T, axis=0)
    imag_part = jnp.sum(lre * rim.T + lim * rre.T, axis=0)
    return jnp.stack([real_part, imag_part])


def local(src_times, momenta, band_offsets, elementals, perambulators):
    tile = elementals.shape[1]
    first_slice = lax.axis_index("src") * tile
    start = src_times[0] - first_slice
    band_total = band_offsets.shape[0] * lax.axis_size("snk")
    reach = band_total // tile
    source_elem = elementals[momenta[0, 0], start]
    pieces = [elementals]
    for step in range(1, reach + 1):
        pieces.append(from_behind(elementals, "src", -step))
    window = jnp.concatenate(pieces, axis=1)[momenta[0, 1]]
    positions = start + band_offsets
    selector = (positions[:, None] == jnp.arange(window.shape[0], dtype=jnp.int32)[None, :]).astype(
        jnp.bfloat16
    )
    sink_elem = jnp.einsum(
        "ow,wxab->oxab", selector, window, preferred_element_type=jnp.float32
    ).astype(jnp.bfloat16)
    terms = jax.vmap(contract, in_axes=(None, 0, 0))(source_elem, sink_elem, perambulators[0])
    partial_sum = jnp.sum(terms, axis=-1)
    total = lax.psum(partial_sum, "spin")
    correlator = total * jnp.float32(ROWS ** (-0.5))
    return (terms[None], correlator[None])


TILE = 4
NEAR, FAR = 0, 1


def fused_kernel(
    times_ref,
    momenta_ref,
    offsets_ref,
    elem_ref,
    tau_ref,
    terms_ref,
    corr_ref,
    tau,
    own,
    win,
    weight,
    left,
    outer,
    tau_sem,
    own_sem,
    put_sem,
    down_send,
    up_send,
    relay_send,
    z_recv,
    x_send,
    x_recv,
    own_send,
    own_recv,
    pair_send,
    pair_recv,
):
    src = lax.axis_index("src")
    x = lax.axis_index("snk")
    z = lax.div(src, 2)
    c = lax.rem(src, 2)
    entries = tau_ref.shape[0]
    other = 1 - x
    sibling = {"src": src + 1 - 2 * c}
    across = {"snk": other}

    def remote(source, target, send, recv, device):
        return pltpu.make_async_remote_copy(
            src_ref=source,
            dst_ref=target,
            send_sem=send,
            recv_sem=recv,
            device_id=device,
            device_id_type=pl.DeviceIdType.MESH,
        )

    def place(kind, k):
        return (2 + 2 * kind + c) * TILE + k

    own_copy = pltpu.make_async_copy(elem_ref, own, own_sem)
    own_copy.start()
    put_copy = pltpu.make_async_copy(elem_ref, win.at[:, pl.ds(c * TILE, TILE)], put_sem)
    put_copy.start()
    for i in range(entries):
        pltpu.make_async_copy(tau_ref.at[i], tau.at[i], tau_sem.at[i]).start()

    barrier = pltpu.get_barrier_semaphore()

    def greet(device):
        pl.semaphore_signal(barrier, inc=1, device_id=device, device_id_type=pl.DeviceIdType.MESH)

    greet(sibling)
    greet(across)
    has_up = z <= 1

    @pl.when(z >= 1)
    def _():
        greet({"src": src - 2})

    @pl.when(z <= 2)
    def _():
        greet({"src": src + 2})

    @pl.when(has_up)
    def _():
        greet({"src": src + 4})

    @pl.when(z >= 2)
    def _():
        greet({"src": src - 4})

    def down(k):
        return remote(
            elem_ref.at[x, k],
            win.at[x, place(NEAR, k)],
            down_send.at[k],
            z_recv.at[NEAR * TILE + k],
            {"src": src - 2},
        )

    def up(k):
        return remote(
            elem_ref.at[x, k],
            win.at[x, place(FAR, k)],
            up_send.at[k],
            z_recv.at[FAR * TILE + k],
            {"src": src + 4},
        )

    def own_push():
        return remote(
            elem_ref, win.at[:, pl.ds(TILE, TILE)], own_send, own_recv, sibling
        )

    def step_of(i):
        first = z <= 1
        odd = lax.rem(i + jnp.where(z == 2, 1, 0), 2)
        kind = jnp.where(first, lax.div(i, TILE), odd)
        k = jnp.where(first, lax.rem(i, TILE), lax.div(i, 2))
        return kind, k

    def wanted(kind, k):
        return (kind == NEAR) | (k < TILE - 1) | (c == 0)

    def feed(i):
        @pl.when((z == 1) | (z == 2))
        def _():
            @pl.when(i == 0)
            def _():
                down(0).start()
                down(1).start()

            @pl.when(i == 1)
            def _():
                down(2).start()

            @pl.when(i == 2)
            def _():
                down(3).start()

        @pl.when(z == 0)
        def _():
            @pl.when(i == 0)
            def _():
                up(0).start()
                up(1).start()

            @pl.when(i == 1)
            def _():
                up(2).start()

            @pl.when(i == 2)
            def _():
                up(3).start()

        @pl.when(z == 1)
        def _():
            @pl.when(i == 3)
            def _():
                relay_down(0).start()
                up(0).start()

            @pl.when(i == 4)
            def _():
                relay_down(1).start()
                relay_down(2).start()
                up(1).start()

            @pl.when(i == 5)
            def _():
                up(2).start()

                @pl.when(c == 0)
                def _():
                    relay_down(3).start()
                    up(3).start()

        @pl.when((z == 3) & (i == 0))
        def _():
            down(0).start()
            down(1).start()
            down(0).wait_send()
            down(2).start()
            down(1).wait_send()
            down(3).start()

    def arrival(kind, k):
        slot = win.at[x, place(kind, k)]
        return remote(slot, slot, x_send.at[0], z_recv.at[kind * TILE + k], across)

    def relay_down(k):
        return remote(
            win.at[x, place(NEAR, k)],
            win.at[x, place(FAR, k)],
            relay_send.at[NEAR * TILE + k],
            z_recv.at[FAR * TILE + k],
            {"src": src - 2},
        )

    def relay_up(k):
        return remote(
            win.at[x, place(FAR, k)],
            win.at[x, place(NEAR, k)],
            relay_send.at[FAR * TILE + k],
            z_recv.at[NEAR * TILE + k],
            {"src": src + 2},
        )

    def cross(kind, k, plane):
        slot = win.at[plane, place(kind, k)]
        at = kind * TILE + k
        return remote(slot, slot, x_send.at[at], x_recv.at[at], across)

    def pair(kind, k, plane, hop):
        slot = win.at[plane, place(kind, k)]
        at = (hop * 2 + kind) * TILE + k
        return remote(slot, slot, pair_send.at[at], pair_recv.at[at], sibling)

    def pair_in(kind, k, plane, hop):
        slot = win.at[plane, (2 + 2 * kind + 1 - c) * TILE + k]
        at = (hop * 2 + kind) * TILE + k
        return remote(slot, slot, pair_send.at[at], pair_recv.at[at], sibling)

    own_copy.wait()
    m0 = momenta_ref[0, 0]
    m1 = momenta_ref[0, 1]
    start = lax.rem(times_ref[0], TILE)
    source = own[m0, start]
    weight[:EIG, :EIG] = source[0]
    weight[:EIG, EIG:] = -source[1]
    weight[EIG:, :EIG] = source[1]
    weight[EIG:, EIG:] = source[0]

    def hand_on(i):
        kind, k = step_of(i)

        @pl.when((kind == NEAR) | (k < TILE - 1) | (c == 0) | (z == 2))
        def _():
            arrival(kind, k).wait_recv()

        @pl.when((kind == NEAR) & (z == 2) & ((c == 0) | (k < TILE - 1)))
        def _():
            relay_down(k).start()

        @pl.when((kind == FAR) & (z == 2))
        def _():
            relay_up(k).start()

        @pl.when(wanted(kind, k))
        def _():
            cross(kind, k, x).start()

        @pl.when((kind == NEAR) | (c == 0))
        def _():
            pair(kind, k, x, 0).start()

    def hand_across(i):
        kind, k = step_of(i)

        @pl.when(wanted(kind, k))
        def _():
            cross(kind, k, other).wait_recv()

        @pl.when((kind == NEAR) | (c == 0))
        def _():
            pair(kind, k, other, 1).start()

    def work(i):
        pltpu.make_async_copy(tau_ref.at[i], tau.at[i], tau_sem.at[i]).wait()
        for a in range(4):
            rows = pl.ds(a * EIG, EIG)
            both = jnp.concatenate([tau[i, 0, rows, :], tau[i, 1, rows, :]], axis=0)
            product = jnp.dot(weight[...], both, preferred_element_type=jnp.float32)
            product = product.astype(jnp.bfloat16)
            left[0, rows, :] = product[:EIG]
            left[1, rows, :] = product[EIG:]
        for p in range(4):
            cols = pl.ds(p * EIG, EIG)
            t = jnp.concatenate([tau[i, 0, :, cols], tau[i, 1, :, cols]], axis=1)
            l = jnp.concatenate([left[0, :, cols], left[1, :, cols]], axis=1)
            q = lax.dot_general(
                t, l, (((0,), (0,)), ((), ())), preferred_element_type=jnp.float32
            )
            outer[i, p, 0] = q[:EIG, :EIG] + q[EIG:, EIG:]
            outer[i, p, 1] = q[:EIG, EIG:] - q[EIG:, :EIG]

    early = jnp.where(z == 0, 3, jnp.where(z == 1, 1, 0))

    @pl.loop(0, early)
    def _(i):
        work(i)

    pl.semaphore_wait(barrier, 4 + jnp.where((z == 1) | (z == 2), 1, 0))

    @pl.loop(0, entries)
    def _(i):
        feed(i)

        @pl.when((c == 1) & (i == 0))
        def _():
            own_push().start()

        hand_on(i)

        @pl.when(i >= 1)
        def _():
            hand_across(i - 1)

        @pl.when(early + i < entries)
        def _():
            work(early + i)

    hand_across(entries - 1)

    put_copy.wait()

    @pl.when(c == 0)
    def _():
        own_push().wait_recv()

    @pl.when(c == 1)
    def _():
        own_push().wait_send()

    for kind in (NEAR, FAR):
        for k in range(TILE):
            if kind == NEAR:
                pair_in(kind, k, x, 0).wait_recv()
                pair_in(kind, k, other, 1).wait_recv()
            else:

                @pl.when(c == 1)
                def _():
                    pair_in(kind, k, x, 0).wait_recv()
                    pair_in(kind, k, other, 1).wait_recv()

    def finish(o):
        sink = win[m1, c * TILE + start + offsets_ref[o]]
        er = sink[0].astype(jnp.float32).T
        ei = sink[1].astype(jnp.float32).T
        for p in range(4):
            mr = outer[o, p, 0]
            mi = outer[o, p, 1]
            cols = pl.ds(p * EIG, EIG)
            terms_ref[o, 0:1, cols] = jnp.sum(er * mr - ei * mi, axis=0, keepdims=True)
            terms_ref[o, 1:2, cols] = jnp.sum(er * mi + ei * mr, axis=0, keepdims=True)

    @pl.loop(0, entries)
    def _(o):
        finish(o)

    corr_ref[...] = jnp.sum(terms_ref[...], axis=-1) * jnp.float32(ROWS ** (-0.5))

    @pl.when((z == 1) | (z == 2))
    def _():
        for k in range(TILE):
            down(k).wait_send()

    @pl.when(z == 3)
    def _():
        down(2).wait_send()
        down(3).wait_send()

    for k in range(TILE):
        last = k == TILE - 1

        @pl.when((z == 0) | ((z == 1) & ((c == 0) | (not last))))
        def _():
            up(k).wait_send()

        @pl.when(((z == 1) | (z == 2)) & ((c == 0) | (not last)))
        def _():
            relay_down(k).wait_send()

        @pl.when(z == 2)
        def _():
            relay_up(k).wait_send()

    for kind in (NEAR, FAR):
        for k in range(TILE):

            @pl.when(wanted(kind, k))
            def _():
                cross(kind, k, x).wait_send()

            if kind == NEAR:
                pair(kind, k, x, 0).wait_send()
                pair(kind, k, other, 1).wait_send()
            else:

                @pl.when(c == 0)
                def _():
                    pair(kind, k, x, 0).wait_send()
                    pair(kind, k, other, 1).wait_send()


def fused_local(src_times, momenta, band_offsets, elementals, perambulators):
    entries = band_offsets.shape[0]
    bf16 = jnp.bfloat16
    dma = pltpu.SemaphoreType.DMA
    smem = pl.BlockSpec(memory_space=pltpu.SMEM)
    hbm = pl.BlockSpec(memory_space=pl.ANY)
    vmem = pl.BlockSpec(memory_space=pltpu.VMEM)
    terms, correlator = pl.pallas_call(
        fused_kernel,
        out_shape=(
            jax.ShapeDtypeStruct((entries, 2, ROWS), jnp.float32),
            jax.ShapeDtypeStruct((entries, 2), jnp.float32),
        ),
        in_specs=[smem, smem, smem, hbm, hbm],
        out_specs=(vmem, vmem),
        scratch_shapes=[
            pltpu.VMEM((entries, 2, ROWS, ROWS), bf16),
            pltpu.VMEM((2, TILE, 2, EIG, EIG), bf16),
            pltpu.VMEM((2, 6 * TILE, 2, EIG, EIG), bf16),
            pltpu.VMEM((2 * EIG, 2 * EIG), bf16),
            pltpu.VMEM((2, ROWS, ROWS), bf16),
            pltpu.VMEM((entries, 4, 2, EIG, EIG), jnp.float32),
            dma((entries,)),
            dma,
            dma,
            dma((TILE,)),
            dma((TILE,)),
            dma((2 * TILE,)),
            dma((2 * TILE,)),
            dma((2 * TILE,)),
            dma((2 * TILE,)),
            dma,
            dma,
            dma((4 * TILE,)),
            dma((4 * TILE,)),
        ],
        compiler_params=pltpu.CompilerParams(
            collective_id=0, has_side_effects=True, vmem_limit_bytes=60 * 1024 * 1024
        ),
        name="band_contraction",
    )(src_times, momenta, band_offsets, elementals, perambulators[0])
    return terms[None], correlator[None]


def solution(mesh):
    placed = (
        P("src"),
        P("src", None),
        P("snk"),
        P("cfg", "src", None, None, None),
        P(("cfg", "src"), "snk", None, None, "spin"),
    )
    inside = local
    if dict(mesh.shape) == {"cfg": 2, "src": 8, "snk": 2, "spin": 1}:
        inside = fused_local
    return jax.shard_map(
        inside,
        mesh=mesh,
        in_specs=placed,
        out_specs=(P(("cfg", "src"), "snk", None, "spin"), P(("cfg", "src"), "snk", None)),
        check_vma=False,
    )
```

```python
import functools

import jax
import jax.numpy as jnp
from jax import lax
from jax.experimental import pallas as pl
from jax.experimental.pallas import tpu as pltpu
from jax.sharding import PartitionSpec as P

EIG = 128
ROWS = 512


def from_behind(value, axis, steps):
    count = lax.axis_size(axis)
    pairs = [(source, (source + steps) % count) for source in range(count)]
    return lax.ppermute(value, axis, pairs)


def contract(source_elem, sink_elem, tau):
    width = tau.shape[-1]
    blocks = tau.reshape(2, 4, EIG, width)

    def rowmul(a, b):
        return jnp.einsum("ab,pbc->pac", a, b, preferred_element_type=jnp.float32).reshape(
            4 * EIG, width
        )

    left_re = (rowmul(source_elem[0], blocks[0]) - rowmul(source_elem[1], blocks[1])).astype(
        jnp.bfloat16
    )
    left_im = (rowmul(source_elem[0], blocks[1]) + rowmul(source_elem[1], blocks[0])).astype(
        jnp.bfloat16
    )
    columns = tau.reshape(2, 4 * EIG, width // EIG, EIG)

    def colmul(a, b):
        return jnp.einsum("ab,iqb->qai", a, b, preferred_element_type=jnp.float32).reshape(
            width, 4 * EIG
        )

    right_re = (colmul(sink_elem[0], columns[0]) + colmul(sink_elem[1], columns[1])).astype(
        jnp.bfloat16
    )
    right_im = (colmul(sink_elem[1], columns[0]) - colmul(sink_elem[0], columns[1])).astype(
        jnp.bfloat16
    )
    lre = left_re.astype(jnp.float32)
    lim = left_im.astype(jnp.float32)
    rre = right_re.astype(jnp.float32)
    rim = right_im.astype(jnp.float32)
    real_part = jnp.sum(lre * rre.T - lim * rim.T, axis=0)
    imag_part = jnp.sum(lre * rim.T + lim * rre.T, axis=0)
    return jnp.stack([real_part, imag_part])


def local(src_times, momenta, band_offsets, elementals, perambulators):
    tile = elementals.shape[1]
    first_slice = lax.axis_index("src") * tile
    start = src_times[0] - first_slice
    band_total = band_offsets.shape[0] * lax.axis_size("snk")
    reach = band_total // tile
    source_elem = elementals[momenta[0, 0], start]
    pieces = [elementals]
    for step in range(1, reach + 1):
        pieces.append(from_behind(elementals, "src", -step))
    window = jnp.concatenate(pieces, axis=1)[momenta[0, 1]]
    positions = start + band_offsets
    selector = (positions[:, None] == jnp.arange(window.shape[0], dtype=jnp.int32)[None, :]).astype(
        jnp.bfloat16
    )
    sink_elem = jnp.einsum(
        "ow,wxab->oxab", selector, window, preferred_element_type=jnp.float32
    ).astype(jnp.bfloat16)
    terms = jax.vmap(contract, in_axes=(None, 0, 0))(source_elem, sink_elem, perambulators[0])
    partial_sum = jnp.sum(terms, axis=-1)
    total = lax.psum(partial_sum, "spin")
    correlator = total * jnp.float32(ROWS ** (-0.5))
    return (terms[None], correlator[None])


TILE = 4
NEAR, FAR = 0, 1


def fused_kernel(
    times_ref,
    momenta_ref,
    offsets_ref,
    elem_ref,
    tau_ref,
    terms_ref,
    corr_ref,
    tau,
    own,
    win,
    weight,
    left,
    outer,
    tau_sem,
    own_sem,
    put_sem,
    down_send,
    up_send,
    relay_send,
    z_recv,
    x_send,
    x_recv,
    own_send,
    own_recv,
    pair_send,
    pair_recv,
):
    src = lax.axis_index("src")
    x = lax.axis_index("snk")
    z = lax.div(src, 2)
    c = lax.rem(src, 2)
    entries = tau_ref.shape[0]
    other = 1 - x
    sibling = {"src": src + 1 - 2 * c}
    across = {"snk": other}

    def remote(source, target, send, recv, device):
        return pltpu.make_async_remote_copy(
            src_ref=source,
            dst_ref=target,
            send_sem=send,
            recv_sem=recv,
            device_id=device,
            device_id_type=pl.DeviceIdType.MESH,
        )

    def place(kind, k):
        return (2 + 2 * kind + c) * TILE + k

    own_copy = pltpu.make_async_copy(elem_ref, own, own_sem)
    own_copy.start()
    put_copy = pltpu.make_async_copy(elem_ref, win.at[:, pl.ds(c * TILE, TILE)], put_sem)
    put_copy.start()
    for i in range(entries):
        pltpu.make_async_copy(tau_ref.at[i], tau.at[i], tau_sem.at[i]).start()

    barrier = pltpu.get_barrier_semaphore()

    def greet(device):
        pl.semaphore_signal(barrier, inc=1, device_id=device, device_id_type=pl.DeviceIdType.MESH)

    greet(sibling)
    greet(across)
    has_up = z <= 1

    @pl.when(z >= 1)
    def _():
        greet({"src": src - 2})

    @pl.when(z <= 2)
    def _():
        greet({"src": src + 2})

    @pl.when(has_up)
    def _():
        greet({"src": src + 4})

    @pl.when(z >= 2)
    def _():
        greet({"src": src - 4})

    def down(k):
        return remote(
            elem_ref.at[x, k],
            win.at[x, place(NEAR, k)],
            down_send.at[k],
            z_recv.at[NEAR * TILE + k],
            {"src": src - 2},
        )

    def up(k):
        return remote(
            elem_ref.at[x, k],
            win.at[x, place(FAR, k)],
            up_send.at[k],
            z_recv.at[FAR * TILE + k],
            {"src": src + 4},
        )

    def own_push():
        return remote(
            elem_ref, win.at[:, pl.ds(TILE, TILE)], own_send, own_recv, sibling
        )

    def step_of(i):
        first = z <= 1
        odd = lax.rem(lax.div(i, 2) + jnp.where(z == 2, 1, 0), 2)
        kind = jnp.where(first, lax.div(i, TILE), odd)
        k = jnp.where(first, lax.rem(i, TILE), lax.div(i, TILE) * 2 + lax.rem(i, 2))
        return kind, k

    def wanted(kind, k):
        return (kind == NEAR) | (k < TILE - 1) | (c == 0)

    def first_batch():
        for k in (0, 1):

            @pl.when(z >= 1)
            def _():
                down(k).start()

            @pl.when(z == 0)
            def _():
                up(k).start()

    def second_batch():
        for k in (0, 1):

            @pl.when(z >= 1)
            def _():
                down(k).wait_send()
                down(k + 2).start()

            @pl.when(z == 0)
            def _():
                up(k).wait_send()
                up(k + 2).start()

            @pl.when(z == 1)
            def _():
                up(k).start()

    def third_batch():
        up(0).wait_send()
        up(2).start()
        up(1).wait_send()

        @pl.when(c == 0)
        def _():
            up(3).start()

    def arrival(kind, k):
        slot = win.at[x, place(kind, k)]
        return remote(slot, slot, x_send.at[0], z_recv.at[kind * TILE + k], across)

    def relay_down(k):
        return remote(
            win.at[x, place(NEAR, k)],
            win.at[x, place(FAR, k)],
            relay_send.at[NEAR * TILE + k],
            z_recv.at[FAR * TILE + k],
            {"src": src - 2},
        )

    def relay_up(k):
        return remote(
            win.at[x, place(FAR, k)],
            win.at[x, place(NEAR, k)],
            relay_send.at[FAR * TILE + k],
            z_recv.at[NEAR * TILE + k],
            {"src": src + 2},
        )

    def cross(kind, k, plane):
        slot = win.at[plane, place(kind, k)]
        at = kind * TILE + k
        return remote(slot, slot, x_send.at[at], x_recv.at[at], across)

    def pair(kind, k, plane, hop):
        slot = win.at[plane, place(kind, k)]
        at = (hop * 2 + kind) * TILE + k
        return remote(slot, slot, pair_send.at[at], pair_recv.at[at], sibling)

    def pair_in(kind, k, plane, hop):
        slot = win.at[plane, (2 + 2 * kind + 1 - c) * TILE + k]
        at = (hop * 2 + kind) * TILE + k
        return remote(slot, slot, pair_send.at[at], pair_recv.at[at], sibling)

    own_copy.wait()
    m0 = momenta_ref[0, 0]
    m1 = momenta_ref[0, 1]
    start = lax.rem(times_ref[0], TILE)
    source = own[m0, start]
    weight[:EIG, :EIG] = source[0]
    weight[:EIG, EIG:] = -source[1]
    weight[EIG:, :EIG] = source[1]
    weight[EIG:, EIG:] = source[0]

    def hand_on(i):
        kind, k = step_of(i)

        @pl.when((kind == NEAR) | (k < TILE - 1) | (c == 0) | (z == 2))
        def _():
            arrival(kind, k).wait_recv()

        @pl.when((kind == NEAR) & ((z == 1) | (z == 2)) & ((c == 0) | (k < TILE - 1)))
        def _():
            relay_down(k).start()

        @pl.when((kind == FAR) & (z == 2))
        def _():
            relay_up(k).start()

        @pl.when(wanted(kind, k))
        def _():
            cross(kind, k, x).start()

        @pl.when((kind == NEAR) | (c == 0))
        def _():
            pair(kind, k, x, 0).start()

    def hand_across(i):
        kind, k = step_of(i)

        @pl.when(wanted(kind, k))
        def _():
            cross(kind, k, other).wait_recv()

        @pl.when((kind == NEAR) | (c == 0))
        def _():
            pair(kind, k, other, 1).start()

    def work(i):
        pltpu.make_async_copy(tau_ref.at[i], tau.at[i], tau_sem.at[i]).wait()
        for a in range(4):
            rows = pl.ds(a * EIG, EIG)
            both = jnp.concatenate([tau[i, 0, rows, :], tau[i, 1, rows, :]], axis=0)
            product = jnp.dot(weight[...], both, preferred_element_type=jnp.float32)
            product = product.astype(jnp.bfloat16)
            left[0, rows, :] = product[:EIG]
            left[1, rows, :] = product[EIG:]
        for p in range(4):
            cols = pl.ds(p * EIG, EIG)
            t = jnp.concatenate([tau[i, 0, :, cols], tau[i, 1, :, cols]], axis=1)
            l = jnp.concatenate([left[0, :, cols], left[1, :, cols]], axis=1)
            q = lax.dot_general(
                t, l, (((0,), (0,)), ((), ())), preferred_element_type=jnp.float32
            )
            outer[i, p, 0] = q[:EIG, :EIG] + q[EIG:, EIG:]
            outer[i, p, 1] = q[:EIG, EIG:] - q[EIG:, :EIG]

    early = jnp.where(z == 0, 3, jnp.where(z == 1, 1, 0))

    @pl.loop(0, early)
    def _(i):
        work(i)

    pl.semaphore_wait(barrier, 4 + jnp.where((z == 1) | (z == 2), 1, 0))

    first_batch()

    @pl.when(c == 1)
    def _():
        own_push().start()

    work(early)
    second_batch()
    ahead = early + 1 + jnp.where(z == 3, 3, 0)

    @pl.loop(early + 1, ahead)
    def _(i):
        work(i)

    @pl.loop(0, entries)
    def _(i):
        hand_on(i)

        @pl.when((z == 1) & (i == 1))
        def _():
            third_batch()

        @pl.when(i >= 2)
        def _():
            hand_across(i - 2)

        @pl.when(ahead + i < entries)
        def _():
            work(ahead + i)

    hand_across(entries - 2)
    hand_across(entries - 1)

    put_copy.wait()

    @pl.when(c == 0)
    def _():
        own_push().wait_recv()

    @pl.when(c == 1)
    def _():
        own_push().wait_send()

    for kind in (NEAR, FAR):
        for k in range(TILE):
            if kind == NEAR:
                pair_in(kind, k, x, 0).wait_recv()
                pair_in(kind, k, other, 1).wait_recv()
            else:

                @pl.when(c == 1)
                def _():
                    pair_in(kind, k, x, 0).wait_recv()
                    pair_in(kind, k, other, 1).wait_recv()

    def finish(o):
        sink = win[m1, c * TILE + start + offsets_ref[o]]
        er = sink[0].astype(jnp.float32).T
        ei = sink[1].astype(jnp.float32).T
        for p in range(4):
            mr = outer[o, p, 0]
            mi = outer[o, p, 1]
            cols = pl.ds(p * EIG, EIG)
            terms_ref[o, 0:1, cols] = jnp.sum(er * mr - ei * mi, axis=0, keepdims=True)
            terms_ref[o, 1:2, cols] = jnp.sum(er * mi + ei * mr, axis=0, keepdims=True)

    @pl.loop(0, entries)
    def _(o):
        finish(o)

    corr_ref[...] = jnp.sum(terms_ref[...], axis=-1) * jnp.float32(ROWS ** (-0.5))

    @pl.when(z >= 1)
    def _():
        down(2).wait_send()
        down(3).wait_send()

    @pl.when(z <= 1)
    def _():
        up(2).wait_send()

    @pl.when((z == 0) | ((z == 1) & (c == 0)))
    def _():
        up(3).wait_send()

    for k in range(TILE):
        last = k == TILE - 1

        @pl.when(((z == 1) | (z == 2)) & ((c == 0) | (not last)))
        def _():
            relay_down(k).wait_send()

        @pl.when(z == 2)
        def _():
            relay_up(k).wait_send()

    for kind in (NEAR, FAR):
        for k in range(TILE):

            @pl.when(wanted(kind, k))
            def _():
                cross(kind, k, x).wait_send()

            if kind == NEAR:
                pair(kind, k, x, 0).wait_send()
                pair(kind, k, other, 1).wait_send()
            else:

                @pl.when(c == 0)
                def _():
                    pair(kind, k, x, 0).wait_send()
                    pair(kind, k, other, 1).wait_send()


def fused_local(src_times, momenta, band_offsets, elementals, perambulators):
    entries = band_offsets.shape[0]
    bf16 = jnp.bfloat16
    dma = pltpu.SemaphoreType.DMA
    smem = pl.BlockSpec(memory_space=pltpu.SMEM)
    hbm = pl.BlockSpec(memory_space=pl.ANY)
    vmem = pl.BlockSpec(memory_space=pltpu.VMEM)
    terms, correlator = pl.pallas_call(
        fused_kernel,
        out_shape=(
            jax.ShapeDtypeStruct((entries, 2, ROWS), jnp.float32),
            jax.ShapeDtypeStruct((entries, 2), jnp.float32),
        ),
        in_specs=[smem, smem, smem, hbm, hbm],
        out_specs=(vmem, vmem),
        scratch_shapes=[
            pltpu.VMEM((entries, 2, ROWS, ROWS), bf16),
            pltpu.VMEM((2, TILE, 2, EIG, EIG), bf16),
            pltpu.VMEM((2, 6 * TILE, 2, EIG, EIG), bf16),
            pltpu.VMEM((2 * EIG, 2 * EIG), bf16),
            pltpu.VMEM((2, ROWS, ROWS), bf16),
            pltpu.VMEM((entries, 4, 2, EIG, EIG), jnp.float32),
            dma((entries,)),
            dma,
            dma,
            dma((TILE,)),
            dma((TILE,)),
            dma((2 * TILE,)),
            dma((2 * TILE,)),
            dma((2 * TILE,)),
            dma((2 * TILE,)),
            dma,
            dma,
            dma((4 * TILE,)),
            dma((4 * TILE,)),
        ],
        compiler_params=pltpu.CompilerParams(
            collective_id=0, has_side_effects=True, vmem_limit_bytes=60 * 1024 * 1024
        ),
        name="band_contraction",
    )(src_times, momenta, band_offsets, elementals, perambulators[0])
    return terms[None], correlator[None]


def solution(mesh):
    placed = (
        P("src"),
        P("src", None),
        P("snk"),
        P("cfg", "src", None, None, None),
        P(("cfg", "src"), "snk", None, None, "spin"),
    )
    inside = local
    if dict(mesh.shape) == {"cfg": 2, "src": 8, "snk": 2, "spin": 1}:
        inside = fused_local
    return jax.shard_map(
        inside,
        mesh=mesh,
        in_specs=placed,
        out_specs=(P(("cfg", "src"), "snk", None, "spin"), P(("cfg", "src"), "snk", None)),
        check_vma=False,
    )
```

```python
import functools

import jax
import jax.numpy as jnp
from jax import lax
from jax.experimental import pallas as pl
from jax.experimental.pallas import tpu as pltpu
from jax.sharding import PartitionSpec as P

EIG = 128
ROWS = 512


def from_behind(value, axis, steps):
    count = lax.axis_size(axis)
    pairs = [(source, (source + steps) % count) for source in range(count)]
    return lax.ppermute(value, axis, pairs)


def contract(source_elem, sink_elem, tau):
    width = tau.shape[-1]
    blocks = tau.reshape(2, 4, EIG, width)

    def rowmul(a, b):
        return jnp.einsum("ab,pbc->pac", a, b, preferred_element_type=jnp.float32).reshape(
            4 * EIG, width
        )

    left_re = (rowmul(source_elem[0], blocks[0]) - rowmul(source_elem[1], blocks[1])).astype(
        jnp.bfloat16
    )
    left_im = (rowmul(source_elem[0], blocks[1]) + rowmul(source_elem[1], blocks[0])).astype(
        jnp.bfloat16
    )
    columns = tau.reshape(2, 4 * EIG, width // EIG, EIG)

    def colmul(a, b):
        return jnp.einsum("ab,iqb->qai", a, b, preferred_element_type=jnp.float32).reshape(
            width, 4 * EIG
        )

    right_re = (colmul(sink_elem[0], columns[0]) + colmul(sink_elem[1], columns[1])).astype(
        jnp.bfloat16
    )
    right_im = (colmul(sink_elem[1], columns[0]) - colmul(sink_elem[0], columns[1])).astype(
        jnp.bfloat16
    )
    lre = left_re.astype(jnp.float32)
    lim = left_im.astype(jnp.float32)
    rre = right_re.astype(jnp.float32)
    rim = right_im.astype(jnp.float32)
    real_part = jnp.sum(lre * rre.T - lim * rim.T, axis=0)
    imag_part = jnp.sum(lre * rim.T + lim * rre.T, axis=0)
    return jnp.stack([real_part, imag_part])


def local(src_times, momenta, band_offsets, elementals, perambulators):
    tile = elementals.shape[1]
    first_slice = lax.axis_index("src") * tile
    start = src_times[0] - first_slice
    band_total = band_offsets.shape[0] * lax.axis_size("snk")
    reach = band_total // tile
    source_elem = elementals[momenta[0, 0], start]
    pieces = [elementals]
    for step in range(1, reach + 1):
        pieces.append(from_behind(elementals, "src", -step))
    window = jnp.concatenate(pieces, axis=1)[momenta[0, 1]]
    positions = start + band_offsets
    selector = (positions[:, None] == jnp.arange(window.shape[0], dtype=jnp.int32)[None, :]).astype(
        jnp.bfloat16
    )
    sink_elem = jnp.einsum(
        "ow,wxab->oxab", selector, window, preferred_element_type=jnp.float32
    ).astype(jnp.bfloat16)
    terms = jax.vmap(contract, in_axes=(None, 0, 0))(source_elem, sink_elem, perambulators[0])
    partial_sum = jnp.sum(terms, axis=-1)
    total = lax.psum(partial_sum, "spin")
    correlator = total * jnp.float32(ROWS ** (-0.5))
    return (terms[None], correlator[None])


TILE = 4
NEAR, FAR = 0, 1


def fused_kernel(
    times_ref,
    momenta_ref,
    offsets_ref,
    elem_ref,
    tau_ref,
    terms_ref,
    corr_ref,
    tau,
    own,
    win,
    weight,
    left,
    outer,
    tau_sem,
    own_sem,
    put_sem,
    down_send,
    up_send,
    relay_send,
    z_recv,
    x_send,
    x_recv,
    own_send,
    own_recv,
    pair_send,
    pair_recv,
):
    src = lax.axis_index("src")
    x = lax.axis_index("snk")
    z = lax.div(src, 2)
    c = lax.rem(src, 2)
    entries = tau_ref.shape[0]
    other = 1 - x
    sibling = {"src": src + 1 - 2 * c}
    across = {"snk": other}

    def remote(source, target, send, recv, device):
        return pltpu.make_async_remote_copy(
            src_ref=source,
            dst_ref=target,
            send_sem=send,
            recv_sem=recv,
            device_id=device,
            device_id_type=pl.DeviceIdType.MESH,
        )

    def place(kind, k):
        return (2 + 2 * kind + c) * TILE + k

    own_copy = pltpu.make_async_copy(elem_ref, own, own_sem)
    own_copy.start()
    put_copy = pltpu.make_async_copy(elem_ref, win.at[:, pl.ds(c * TILE, TILE)], put_sem)
    put_copy.start()
    for i in range(entries):
        pltpu.make_async_copy(tau_ref.at[i], tau.at[i], tau_sem.at[i]).start()

    barrier = pltpu.get_barrier_semaphore()

    def greet(device):
        pl.semaphore_signal(barrier, inc=1, device_id=device, device_id_type=pl.DeviceIdType.MESH)

    greet(sibling)
    greet(across)
    has_up = z <= 1

    @pl.when(z >= 1)
    def _():
        greet({"src": src - 2})

    @pl.when(z <= 2)
    def _():
        greet({"src": src + 2})

    @pl.when(has_up)
    def _():
        greet({"src": src + 4})

    @pl.when(z >= 2)
    def _():
        greet({"src": src - 4})

    def down(k):
        return remote(
            elem_ref.at[x, k],
            win.at[x, place(NEAR, k)],
            down_send.at[k],
            z_recv.at[NEAR * TILE + k],
            {"src": src - 2},
        )

    def up(k):
        return remote(
            elem_ref.at[x, k],
            win.at[x, place(FAR, k)],
            up_send.at[k],
            z_recv.at[FAR * TILE + k],
            {"src": src + 4},
        )

    def own_push():
        return remote(
            elem_ref, win.at[:, pl.ds(TILE, TILE)], own_send, own_recv, sibling
        )

    def step_of(i):
        first = z <= 1
        odd = lax.rem(lax.div(i, 2) + jnp.where(z == 3, 1, 0), 2)
        kind = jnp.where(first, lax.div(i, TILE), odd)
        k = jnp.where(first, lax.rem(i, TILE), lax.div(i, TILE) * 2 + lax.rem(i, 2))
        return kind, k

    def wanted(kind, k):
        return (kind == NEAR) | (k < TILE - 1) | (c == 0)

    def first_batch():
        for k in (0, 1):

            @pl.when(z >= 1)
            def _():
                down(k).start()

            @pl.when(z <= 1)
            def _():
                up(k).start()

    def second_batch():
        for k in (0, 1):

            @pl.when(z >= 1)
            def _():
                down(k).wait_send()
                down(k + 2).start()

            @pl.when(z == 0)
            def _():
                up(k).wait_send()
                up(k + 2).start()

    def third_batch():
        up(0).wait_send()
        up(2).start()
        up(1).wait_send()

        @pl.when(c == 0)
        def _():
            up(3).start()

    def arrival(kind, k):
        slot = win.at[x, place(kind, k)]
        return remote(slot, slot, x_send.at[0], z_recv.at[kind * TILE + k], across)

    def relay_down(k):
        return remote(
            win.at[x, place(NEAR, k)],
            win.at[x, place(FAR, k)],
            relay_send.at[NEAR * TILE + k],
            z_recv.at[FAR * TILE + k],
            {"src": src - 2},
        )

    def relay_up(k):
        return remote(
            win.at[x, place(FAR, k)],
            win.at[x, place(NEAR, k)],
            relay_send.at[FAR * TILE + k],
            z_recv.at[NEAR * TILE + k],
            {"src": src + 2},
        )

    def cross(kind, k, plane):
        slot = win.at[plane, place(kind, k)]
        at = kind * TILE + k
        return remote(slot, slot, x_send.at[at], x_recv.at[at], across)

    def pair(kind, k, plane, hop):
        slot = win.at[plane, place(kind, k)]
        at = (hop * 2 + kind) * TILE + k
        return remote(slot, slot, pair_send.at[at], pair_recv.at[at], sibling)

    def pair_in(kind, k, plane, hop):
        slot = win.at[plane, (2 + 2 * kind + 1 - c) * TILE + k]
        at = (hop * 2 + kind) * TILE + k
        return remote(slot, slot, pair_send.at[at], pair_recv.at[at], sibling)

    own_copy.wait()
    m0 = momenta_ref[0, 0]
    m1 = momenta_ref[0, 1]
    start = lax.rem(times_ref[0], TILE)
    source = own[m0, start]
    weight[:EIG, :EIG] = source[0]
    weight[:EIG, EIG:] = -source[1]
    weight[EIG:, :EIG] = source[1]
    weight[EIG:, EIG:] = source[0]

    def hand_on(i):
        kind, k = step_of(i)

        @pl.when((kind == NEAR) | (k < TILE - 1) | (c == 0) | (z == 2))
        def _():
            arrival(kind, k).wait_recv()

        @pl.when((kind == NEAR) & ((z == 1) | (z == 2)) & ((c == 0) | (k < TILE - 1)))
        def _():
            relay_down(k).start()

        @pl.when((kind == FAR) & (z == 2))
        def _():
            relay_up(k).start()

        @pl.when(wanted(kind, k))
        def _():
            cross(kind, k, x).start()

        @pl.when((kind == NEAR) | (c == 0))
        def _():
            pair(kind, k, x, 0).start()

    def hand_across(i):
        kind, k = step_of(i)

        @pl.when(wanted(kind, k))
        def _():
            cross(kind, k, other).wait_recv()

        @pl.when((kind == NEAR) | (c == 0))
        def _():
            pair(kind, k, other, 1).start()

    def work(i):
        pltpu.make_async_copy(tau_ref.at[i], tau.at[i], tau_sem.at[i]).wait()
        for a in range(4):
            rows = pl.ds(a * EIG, EIG)
            both = jnp.concatenate([tau[i, 0, rows, :], tau[i, 1, rows, :]], axis=0)
            product = jnp.dot(weight[...], both, preferred_element_type=jnp.float32)
            product = product.astype(jnp.bfloat16)
            left[0, rows, :] = product[:EIG]
            left[1, rows, :] = product[EIG:]
        for p in range(4):
            cols = pl.ds(p * EIG, EIG)
            t = jnp.concatenate([tau[i, 0, :, cols], tau[i, 1, :, cols]], axis=1)
            l = jnp.concatenate([left[0, :, cols], left[1, :, cols]], axis=1)
            q = lax.dot_general(
                t, l, (((0,), (0,)), ((), ())), preferred_element_type=jnp.float32
            )
            outer[i, p, 0] = q[:EIG, :EIG] + q[EIG:, EIG:]
            outer[i, p, 1] = q[:EIG, EIG:] - q[EIG:, :EIG]

    early = jnp.where(z == 0, 3, jnp.where(z == 1, 1, 0))

    @pl.loop(0, early)
    def _(i):
        work(i)

    pl.semaphore_wait(barrier, 4 + jnp.where((z == 1) | (z == 2), 1, 0))

    first_batch()

    @pl.when(c == 1)
    def _():
        own_push().start()

    work(early)
    second_batch()
    ahead = early + 1 + jnp.where(z == 3, 5, 0)

    @pl.loop(early + 1, ahead)
    def _(i):
        work(i)

    @pl.loop(0, entries)
    def _(i):
        hand_on(i)

        @pl.when((z == 1) & (i == 1))
        def _():
            third_batch()

        @pl.when(i >= 2)
        def _():
            hand_across(i - 2)

        @pl.when(ahead + i < entries)
        def _():
            work(ahead + i)

    hand_across(entries - 2)
    hand_across(entries - 1)

    put_copy.wait()

    @pl.when(c == 0)
    def _():
        own_push().wait_recv()

    @pl.when(c == 1)
    def _():
        own_push().wait_send()

    for kind in (NEAR, FAR):
        for k in range(TILE):
            if kind == NEAR:
                pair_in(kind, k, x, 0).wait_recv()
                pair_in(kind, k, other, 1).wait_recv()
            else:

                @pl.when(c == 1)
                def _():
                    pair_in(kind, k, x, 0).wait_recv()
                    pair_in(kind, k, other, 1).wait_recv()

    def finish(o):
        sink = win[m1, c * TILE + start + offsets_ref[o]]
        er = sink[0].astype(jnp.float32).T
        ei = sink[1].astype(jnp.float32).T
        for p in range(4):
            mr = outer[o, p, 0]
            mi = outer[o, p, 1]
            cols = pl.ds(p * EIG, EIG)
            terms_ref[o, 0:1, cols] = jnp.sum(er * mr - ei * mi, axis=0, keepdims=True)
            terms_ref[o, 1:2, cols] = jnp.sum(er * mi + ei * mr, axis=0, keepdims=True)

    @pl.loop(0, entries)
    def _(o):
        finish(o)

    corr_ref[...] = jnp.sum(terms_ref[...], axis=-1) * jnp.float32(ROWS ** (-0.5))

    @pl.when(z >= 1)
    def _():
        down(2).wait_send()
        down(3).wait_send()

    @pl.when(z <= 1)
    def _():
        up(2).wait_send()

    @pl.when((z == 0) | ((z == 1) & (c == 0)))
    def _():
        up(3).wait_send()

    for k in range(TILE):
        last = k == TILE - 1

        @pl.when(((z == 1) | (z == 2)) & ((c == 0) | (not last)))
        def _():
            relay_down(k).wait_send()

        @pl.when(z == 2)
        def _():
            relay_up(k).wait_send()

    for kind in (NEAR, FAR):
        for k in range(TILE):

            @pl.when(wanted(kind, k))
            def _():
                cross(kind, k, x).wait_send()

            if kind == NEAR:
                pair(kind, k, x, 0).wait_send()
                pair(kind, k, other, 1).wait_send()
            else:

                @pl.when(c == 0)
                def _():
                    pair(kind, k, x, 0).wait_send()
                    pair(kind, k, other, 1).wait_send()


def fused_local(src_times, momenta, band_offsets, elementals, perambulators):
    entries = band_offsets.shape[0]
    bf16 = jnp.bfloat16
    dma = pltpu.SemaphoreType.DMA
    smem = pl.BlockSpec(memory_space=pltpu.SMEM)
    hbm = pl.BlockSpec(memory_space=pl.ANY)
    vmem = pl.BlockSpec(memory_space=pltpu.VMEM)
    terms, correlator = pl.pallas_call(
        fused_kernel,
        out_shape=(
            jax.ShapeDtypeStruct((entries, 2, ROWS), jnp.float32),
            jax.ShapeDtypeStruct((entries, 2), jnp.float32),
        ),
        in_specs=[smem, smem, smem, hbm, hbm],
        out_specs=(vmem, vmem),
        scratch_shapes=[
            pltpu.VMEM((entries, 2, ROWS, ROWS), bf16),
            pltpu.VMEM((2, TILE, 2, EIG, EIG), bf16),
            pltpu.VMEM((2, 6 * TILE, 2, EIG, EIG), bf16),
            pltpu.VMEM((2 * EIG, 2 * EIG), bf16),
            pltpu.VMEM((2, ROWS, ROWS), bf16),
            pltpu.VMEM((entries, 4, 2, EIG, EIG), jnp.float32),
            dma((entries,)),
            dma,
            dma,
            dma((TILE,)),
            dma((TILE,)),
            dma((2 * TILE,)),
            dma((2 * TILE,)),
            dma((2 * TILE,)),
            dma((2 * TILE,)),
            dma,
            dma,
            dma((4 * TILE,)),
            dma((4 * TILE,)),
        ],
        compiler_params=pltpu.CompilerParams(
            collective_id=0, has_side_effects=True, vmem_limit_bytes=60 * 1024 * 1024
        ),
        name="band_contraction",
    )(src_times, momenta, band_offsets, elementals, perambulators[0])
    return terms[None], correlator[None]


def solution(mesh):
    placed = (
        P("src"),
        P("src", None),
        P("snk"),
        P("cfg", "src", None, None, None),
        P(("cfg", "src"), "snk", None, None, "spin"),
    )
    inside = local
    if dict(mesh.shape) == {"cfg": 2, "src": 8, "snk": 2, "spin": 1}:
        inside = fused_local
    return jax.shard_map(
        inside,
        mesh=mesh,
        in_specs=placed,
        out_specs=(P(("cfg", "src"), "snk", None, "spin"), P(("cfg", "src"), "snk", None)),
        check_vma=False,
    )
```
